32 devices in a mesh: tm: 8 (over y, x, core), freq: 4 (over z).
Axes of the slice: x: 2, y: 2, z: 4, core: 2. Of those that a mesh axis runs over, the one named last changes fastest.
Arguments:
- records: bfloat16 [524288, 1024], P('tm', 'freq'), may hold values from -6 to 6
- bins: int32 [32], P('freq'), may hold values from 0 to 4095, as said below
- loads: bfloat16 [2, 64, 1024], P(None, None, 'tm'), may hold values from -0.1875 to 0.1875
Outputs:
- csd: float32 [1024, 32, 2, 1024], P('tm', 'freq')
- psd: float32 [2, 32, 64, 64], P(None, 'freq', 'tm')
The draws below stay inside these ranges and needn't reach their ends.
Inputs may be any that keep to these rules, and one draw needn't show every extreme that they name: The 32 entries are distinct; entries 8 f to 8 (f + 1) - 1 are the bins owned by index f of freq.
All inputs are finite; a program needn't handle non-finite values.
Results may differ from the reference program's by a relative error of at most 0.0048.
Values may be sent and summed in bfloat16 or wider, within the bound.
A program may use at most 320 MiB of HBM per device.

```python
import math
import jax
import jax.numpy as jnp
from jax import lax

C = 1024
SEGLEN = 8192
LOADS = 64
SEG = 16
NBINS = 32
HOP = 4096
SAMPLES = 524288
N_TM = 8


def draw_bins(key, part):
    key = jax.random.fold_in(key, 5)
    inner = jax.random.permutation(key, HOP - 2)[:NBINS - 2] + 1
    ends = jnp.array([0, HOP - 1], jnp.int32)
    both = jnp.concatenate([ends, inner.astype(jnp.int32)])
    return jax.random.permutation(jax.random.fold_in(key, 1), both).astype(jnp.int32)


def steps_of(stream_key, shape, pieces, low, largest):
    gain = 1.0
    for axis_at, blocks in pieces:
        steps = jax.random.uniform(jax.random.fold_in(jax.random.fold_in(stream_key, 6), axis_at), (blocks,), jnp.float32, low / len(pieces), largest / len(pieces))
        gain = gain * jnp.repeat(jnp.exp(steps), shape[axis_at] // blocks).reshape((-1,) + (1,) * (len(shape) - 1 - axis_at))
    return gain


def noise(own_key, shape, spread, most, split=(), kind=jnp.bfloat16):
    values = spread * jax.random.normal(own_key, shape, jnp.float32)
    if split:
        values = values * steps_of(own_key, shape, split, -0.22, 0.18)
    return jnp.clip(values, -most, most).astype(kind)


def setup_inputs(seed: int = 0) -> dict:
    seeds = jax.random.split(jax.random.key(seed), 4)
    records = noise(seeds[0], (SAMPLES, C), 1.0, 6.0, ((0, 8), (1, 4)))
    bins = draw_bins(jax.random.fold_in(seeds[3], 71), 0)
    loads = noise(seeds[2], (2, LOADS, C), C ** -0.5, 0.1875, ((2, 8),))
    return {"records": records, "bins": bins, "loads": loads}


def make_table(bin_ids):
    positions = lax.iota(jnp.int32, SEGLEN)
    turns = (bin_ids.astype(jnp.int32)[:, None] * positions[None, :]) % SEGLEN
    angle = (2.0 * math.pi / SEGLEN) * turns.astype(jnp.float32)
    window = 0.5 - 0.5 * jnp.cos((2.0 * math.pi / SEGLEN) * positions.astype(jnp.float32))
    table = jnp.concatenate([window[None, :] * jnp.cos(angle), -window[None, :] * jnp.sin(angle)], axis=0)
    return table.astype(jnp.bfloat16), jnp.sum(window * window)


def reference(records, bins, loads):
    highest = lax.Precision.HIGHEST
    table, energy = make_table(bins)
    half = SEGLEN // 2
    total = records.shape[0]
    front = table[:, :half].astype(jnp.float32)
    back = table[:, half:].astype(jnp.float32)

    def block(index):
        start = (index * (SEG * half)).astype(jnp.int32)
        piece = lax.dynamic_slice_in_dim(records, start, SEG * half, 0).astype(jnp.float32)
        piece = piece.reshape(SEG, half, C)
        later = jnp.minimum(start + SEG * half, total - half).astype(jnp.int32)
        following = lax.dynamic_slice_in_dim(records, later, half, 0).astype(jnp.float32)
        following = jnp.where(index < N_TM - 1, following, jnp.zeros_like(following))
        seconds = jnp.concatenate([piece[1:], following[None]], axis=0)
        spec = jnp.einsum("kn,snc->skc", front, piece, precision=highest)
        spec = spec + jnp.einsum("kn,snc->skc", back, seconds, precision=highest)
        return spec.astype(jnp.bfloat16)

    spectra = lax.map(block, jnp.arange(N_TM, dtype=jnp.int32))
    spectra = spectra.reshape(N_TM * SEG, 2, NBINS, C).astype(jnp.float32)
    turned = jnp.stack([spectra[:, 1], -spectra[:, 0]], axis=1)
    real = jnp.einsum("spbi,spbj->ibj", spectra, spectra, precision=highest)
    imag = jnp.einsum("spbi,spbj->ibj", turned, spectra, precision=highest)
    scale = 1.0 / (SEG * N_TM * energy)
    csd = jnp.stack([real, imag], axis=2) * scale
    whole = loads.astype(jnp.float32)
    q_real = jnp.einsum("ibj,mj->ibm", csd[:, :, 0], whole[0], precision=highest) + jnp.einsum("ibj,mj->ibm", csd[:, :, 1], whole[1], precision=highest)
    q_imag = jnp.einsum("ibj,mj->ibm", csd[:, :, 1], whole[0], precision=highest) - jnp.einsum("ibj,mj->ibm", csd[:, :, 0], whole[1], precision=highest)
    p_real = jnp.einsum("li,ibm->blm", whole[0], q_real, precision=highest) - jnp.einsum("li,ibm->blm", whole[1], q_imag, precision=highest)
    p_imag = jnp.einsum("li,ibm->blm", whole[0], q_imag, precision=highest) + jnp.einsum("li,ibm->blm", whole[1], q_real, precision=highest)
    psd = jnp.stack([p_real, p_imag], axis=0)
    return csd, psd
```

```python
import math

import jax
import jax.numpy as jnp
from jax import lax
from jax.sharding import PartitionSpec as P

SEGLEN = 8192


def shifted(value, axis, steps):
    count = lax.axis_size(axis)
    first, last = (max(0, -steps), min(count, count - steps))
    return lax.ppermute(value, axis, [(source, source + steps) for source in range(first, last)])


def make_table(bin_ids):
    step = 2.0 * math.pi / SEGLEN
    low = lax.iota(jnp.int32, 128)
    high = lax.iota(jnp.int32, SEGLEN // 128) * 128
    low_angle = step * (bin_ids[:, None] * low[None, :] % SEGLEN).astype(jnp.float32)
    high_angle = step * (bin_ids[:, None] * high[None, :] % SEGLEN).astype(jnp.float32)
    cl, sl = jnp.cos(low_angle)[:, None, :], jnp.sin(low_angle)[:, None, :]
    ch, sh = jnp.cos(high_angle)[:, :, None], jnp.sin(high_angle)[:, :, None]
    window = 0.5 - 0.5 * jnp.cos(step * lax.iota(jnp.int32, SEGLEN).astype(jnp.float32))
    win = window.reshape(1, -1, 128)
    real = win * (ch * cl - sh * sl)
    imag = -win * (sh * cl + ch * sl)
    table = jnp.concatenate([real, imag], axis=0).astype(jnp.bfloat16)
    return (table.reshape(-1, 2, SEGLEN // 2), jnp.sum(window * window))


def per_device(records, bins, loads):
    highest = lax.Precision.HIGHEST
    tm_count = lax.axis_size("tm")
    all_bins = lax.all_gather(bins, "freq", axis=0, tiled=True)
    whole = lax.all_gather(loads, "tm", axis=2, tiled=True)
    table, energy = make_table(all_bins)
    half = SEGLEN // 2
    chans = records.shape[1]
    segs = records.shape[0] // half
    nbins = all_bins.shape[0]
    halves = records.reshape(segs, half, chans)
    both = jnp.concatenate([table[:, 0], table[:, 1]], axis=0)
    terms = jnp.einsum("kn,snc->skc", both, halves, preferred_element_type=jnp.float32)
    front, back = terms[:, : 2 * nbins], terms[:, 2 * nbins :]
    following = shifted(back[0], "tm", -1)
    spec = front + jnp.concatenate([back[1:], following[None]], axis=0)
    spectra = spec.reshape(segs, 2, nbins, chans).astype(jnp.bfloat16)
    owned = lax.all_to_all(spectra, "freq", split_axis=2, concat_axis=3, tiled=True)
    everything = lax.all_gather(owned, "tm", axis=0, tiled=True)
    rows = loads.shape[2]
    mine = lax.dynamic_slice_in_dim(everything, lax.axis_index("tm") * rows, rows, 3)
    scale = 1.0 / (segs * tm_count * energy)
    turned = jnp.stack([mine[:, 1], -mine[:, 0]], axis=1)
    left = jnp.stack([mine, turned], axis=0)
    csd = jnp.einsum("rspbi,spbj->ibrj", left, everything, preferred_element_type=jnp.float32) * scale
    hx_ra = jnp.einsum("hmj,spbj->hspbm", whole, everything, preferred_element_type=jnp.float32)
    y_real = hx_ra[0, :, 0] - hx_ra[1, :, 1]
    y_imag = hx_ra[0, :, 1] + hx_ra[1, :, 0]
    y = jnp.stack([y_real, y_imag], axis=1)
    count = y.shape[3] // tm_count
    ym = lax.dynamic_slice_in_dim(y, lax.axis_index("tm") * count, count, 3)
    yt = jnp.stack([ym, jnp.stack([ym[:, 1], -ym[:, 0]], axis=1)], axis=0)
    psd = jnp.einsum("rspbl,spbm->rblm", yt, y, precision=highest) * scale
    return (csd, psd)


def solution(mesh):
    placed = (P("tm", "freq"), P("freq"), P(None, None, "tm"))
    return jax.shard_map(
        per_device,
        mesh=mesh,
        in_specs=placed,
        out_specs=(P("tm", "freq", None, None), P(None, "freq", "tm", None)),
        check_vma=False,
    )
```

```python
import functools
import math

import jax
import jax.numpy as jnp
import numpy as np
from jax import lax
from jax.experimental import pallas as pl
from jax.experimental.pallas import tpu as pltpu
from jax.sharding import PartitionSpec as P

SEGLEN = 8192
HALF = SEGLEN // 2
MESH = pl.DeviceIdType.MESH
MIB = 1 << 20


def window_of():
    return 0.5 - 0.5 * np.cos(2.0 * np.pi / SEGLEN * np.arange(SEGLEN))


def flipped(index, bits):
    for bit in bits:
        index = index + bit * (1 - 2 * ((index // bit) % 2))
    return index


def bits_of(number):
    return [1 << at for at in range(number.bit_length()) if number >> at & 1]


def spectra_kernel(
    shape, records_ref, bins_ref, loads_ref, window_ref, out_ref, all_loads_ref,
    rec, all_bins, table, front, halo_out, halo, spec, gathered, loads_buf,
    rec_sem, bin_send, bin_recv, load_send, load_recv, halo_sems, local_sem,
    z_send, z_recv, t_send, t_recv, out_sem, loads_sem,
):
    times, freqs, segs, own, chans, chunks = shape
    t, f = lax.axis_index("tm"), lax.axis_index("freq")
    rows = freqs * 2 * own
    size = segs // chunks

    def fetch(j):
        start = j * HALF if isinstance(j, int) else pl.multiple_of(j * HALF, HALF)
        return pltpu.make_async_copy(records_ref.at[pl.ds(start, HALF)], rec.at[j], rec_sem.at[j])

    for j in range(segs):
        fetch(j).start()

    row = lax.broadcasted_iota(jnp.int32, (own, 128), 0)
    held_bins = jnp.zeros((own, 128), jnp.int32)
    for q in range(own):
        held_bins = jnp.where(row == q, bins_ref[q], held_bins)
    all_bins[f] = held_bins
    held_rows = loads_ref.shape[1]
    if held_rows % 128:
        loads_slot = loads_buf.at[t]
    else:
        loads_slot = loads_buf.at[:, pl.ds(pl.multiple_of(t * held_rows, held_rows), held_rows)]

    barrier = pltpu.get_barrier_semaphore()
    for d in range(1, times):
        pl.semaphore_signal(barrier, inc=1, device_id={"tm": lax.rem(t + d, times)}, device_id_type=MESH)
    for e in range(1, freqs):
        pl.semaphore_signal(barrier, inc=1, device_id={"freq": lax.rem(f + e, freqs)}, device_id_type=MESH)
    pl.semaphore_wait(barrier, times + freqs - 2)

    sends = []
    bin_copies = []
    for e in range(1, freqs):
        copy = pltpu.make_async_remote_copy(
            all_bins.at[f], all_bins.at[f], bin_send.at[e], bin_recv.at[e],
            device_id={"freq": lax.rem(f + e, freqs)}, device_id_type=MESH)
        copy.start()
        bin_copies.append(copy)
    load_copies = []
    for d in range(1, times):
        copy = pltpu.make_async_remote_copy(
            loads_ref, loads_slot, load_send.at[d], load_recv.at[d],
            device_id={"tm": lax.rem(t + d, times)}, device_id_type=MESH)
        copy.start()
        load_copies.append(copy)
    loads_slot[...] = loads_ref[...]

    @pl.when(t == times - 1)
    def _():
        halo[...] = jnp.zeros_like(halo)

    for copy in bin_copies:
        copy.wait()

    step = 2.0 * math.pi / SEGLEN
    ks = all_bins[...].reshape(freqs * own, 128)
    lane = lax.broadcasted_iota(jnp.int32, ks.shape, 1)
    low = step * ((ks * lane) & (SEGLEN - 1)).astype(jnp.float32)
    high = step * ((ks * lane * 128) & (SEGLEN - 1)).astype(jnp.float32)
    cl, sl, ch, sh = jnp.cos(low), jnp.sin(low), jnp.cos(high), jnp.sin(high)
    blocks = HALF // 128
    for h in range(2 * blocks):
        w = window_ref[h : h + 1, :]
        c1, s1 = ch[:, h : h + 1], sh[:, h : h + 1]
        real = w * (c1 * cl - s1 * sl)
        imag = -w * (s1 * cl + c1 * sl)
        parts = jnp.concatenate(
            [real.reshape(freqs, 1, own, 128), imag.reshape(freqs, 1, own, 128)], axis=1
        ).reshape(rows, 128)
        at = h // blocks * rows
        table[at : at + rows, h % blocks * 128 : (h % blocks + 1) * 128] = parts.astype(jnp.bfloat16)

    def transform(j):
        fetch(j).wait()
        return jnp.dot(table[...], rec[j], preferred_element_type=jnp.float32)

    def keep(j, value):
        value = value.astype(jnp.bfloat16)
        for g in range(freqs):
            spec[g, j] = value[g * 2 * own : (g + 1) * 2 * own]

    first = transform(0)
    front[...] = first[:rows]
    halo_out[...] = first[rows:]

    def halo_copy():
        return pltpu.make_async_remote_copy(
            halo_out, halo, halo_sems.at[0], halo_sems.at[1],
            device_id={"tm": jnp.maximum(t - 1, 0)}, device_id_type=MESH)

    @pl.when(t > 0)
    def _():
        halo_copy().start()

    def body(j, carry):
        terms = transform(j)
        keep(j - 1, front[...] + terms[rows:])
        front[...] = terms[:rows]
        return carry

    columns = pl.ds(pl.multiple_of(f * chans, chans), chans)
    highs = [1 << at for at in range(1, (times - 1).bit_length())]
    orders = []
    for c in range(chunks):
        turn = c % max(len(highs), 1)
        orders.append(highs[turn:] + highs[:turn] + [1])
    stages = len(orders[0])

    def span(c):
        return pl.ds(c * size, size)

    z_copies, t_copies, locals_ = {}, {}, {}

    def send_t(c, held, bit):
        block = gathered.at[flipped(t, bits_of(held)), span(c)]
        copy = pltpu.make_async_remote_copy(
            block, block, t_send.at[c, held | bit], t_recv.at[c, held | bit],
            device_id={"tm": flipped(t, [bit])}, device_id_type=MESH)
        copy.start()
        t_copies[c, held | bit] = copy

    def top(order, held):
        return max(at for at, bit in enumerate(order) if held & bit)

    for at in range(chunks + stages + 1):
        if at < chunks:
            c = at
            lax.fori_loop(c * size + 1, min((c + 1) * size, segs - 1) + 1, body, 0)
            if c == chunks - 1:
                @pl.when(t < times - 1)
                def _():
                    halo_copy().wait_recv()
                keep(segs - 1, front[...] + halo[...])
            for e in range(1, freqs):
                peer = lax.rem(f + e, freqs)
                copy = pltpu.make_async_remote_copy(
                    spec.at[peer, span(c)], gathered.at[t, span(c), :, columns],
                    z_send.at[c, e], z_recv.at[c, e],
                    device_id={"freq": peer}, device_id_type=MESH)
                copy.start()
                z_copies[c, e] = copy
            locals_[c] = pltpu.make_async_copy(
                spec.at[f, span(c)], gathered.at[t, span(c), :, columns], local_sem.at[c])
            locals_[c].start()
        for c in range(chunks):
            stage = at - 1 - c
            if stage < 0 or stage > stages:
                continue
            order = orders[c]
            if stage == 0:
                locals_[c].wait()
                for e in range(1, freqs):
                    z_copies[c, e].wait_recv()
                for bit in order:
                    send_t(c, 0, bit)
                continue
            for held in range(1, times):
                if top(order, held) == stage - 1:
                    t_copies[c, held].wait_recv()
                    for bit in order[stage:]:
                        send_t(c, held, bit)
            if stage == stages:
                pltpu.make_async_copy(gathered.at[:, span(c)], out_ref.at[:, span(c)], out_sem.at[c]).start()

    for copy in load_copies:
        copy.wait()
    loads_out = pltpu.make_async_copy(loads_buf, all_loads_ref, loads_sem)
    loads_out.start()

    @pl.when(t > 0)
    def _():
        halo_copy().wait_send()

    for copy in list(z_copies.values()) + list(t_copies.values()):
        copy.wait_send()
    for c in range(chunks):
        pltpu.make_async_copy(gathered.at[:, span(c)], out_ref.at[:, span(c)], out_sem.at[c]).wait()
    loads_out.wait()


def gather_spectra(records, bins, loads):
    times, freqs = lax.axis_size("tm"), lax.axis_size("freq")
    segs, own, chans = records.shape[0] // HALF, bins.shape[0], records.shape[1]
    chunks = 4
    rows = freqs * 2 * own
    count, held = 2 * loads.shape[1], loads.shape[2]
    gathered_loads = (times, count, held) if held % 128 else (count, times * held)
    window = jnp.asarray(window_of().reshape(-1, 128), jnp.float32)
    dma = pltpu.SemaphoreType.DMA
    smem = pl.BlockSpec(memory_space=pltpu.SMEM)
    anywhere, vmem = pl.BlockSpec(memory_space=pl.ANY), pl.BlockSpec(memory_space=pltpu.VMEM)
    return pl.pallas_call(
        functools.partial(spectra_kernel, (times, freqs, segs, own, chans, chunks)),
        out_shape=(
            jax.ShapeDtypeStruct((times, segs, 2 * own, freqs * chans), jnp.bfloat16),
            jax.ShapeDtypeStruct(gathered_loads, jnp.bfloat16),
        ),
        in_specs=[anywhere, smem, vmem, vmem],
        out_specs=(anywhere, anywhere),
        scratch_shapes=[
            pltpu.VMEM((segs, HALF, chans), jnp.bfloat16),
            pltpu.VMEM((freqs, own, 128), jnp.int32),
            pltpu.VMEM((2 * rows, HALF), jnp.bfloat16),
            pltpu.VMEM((rows, chans), jnp.float32),
            pltpu.VMEM((rows, chans), jnp.float32),
            pltpu.VMEM((rows, chans), jnp.float32),
            pltpu.VMEM((freqs, segs, 2 * own, chans), jnp.bfloat16),
            pltpu.VMEM((times, segs, 2 * own, freqs * chans), jnp.bfloat16),
            pltpu.VMEM(gathered_loads, jnp.bfloat16),
            dma((segs,)), dma((freqs,)), dma((freqs,)), dma((times,)), dma((times,)), dma((2,)), dma((chunks,)),
            dma((chunks, freqs)), dma((chunks, freqs)), dma((chunks, times)), dma((chunks, times)),
            dma((chunks,)), dma(()),
        ],
        compiler_params=pltpu.CompilerParams(
            collective_id=0, has_side_effects=True, vmem_limit_bytes=56 * MIB),
        name="spectra",
    )(records, bins, loads.reshape(count, -1), window)


def csd_kernel(scale, own, all_ref, loads_ref, mine_ref, csd_ref, psd_ref, wide, wide_mine, applied, held):
    b = pl.program_id(0)
    tiles, depth = wide.shape[0], wide.shape[1] // (2 * own)
    rows, count = csd_ref.shape[0], loads_ref.shape[0] // 2
    over_rows = (((0,), (0,)), ((), ()))

    @pl.when(b == 0)
    def _():
        for c in range(tiles):
            wide[c] = all_ref[:, c * 128 : (c + 1) * 128].astype(jnp.float32)
        if wide_mine is not None:
            wide_mine[...] = mine_ref[...].astype(jnp.float32)
        applied[...] = lax.dot_general(
            all_ref[...], loads_ref[...], (((1,), (1,)), ((), ())), preferred_element_type=jnp.float32)

    real_at, imag_at = pl.ds(b, depth, stride=2 * own), pl.ds(own + b, depth, stride=2 * own)
    t = lax.axis_index("tm")
    if wide_mine is None:
        mine_a, mine_b = wide[t, real_at, :], wide[t, imag_at, :]
    else:
        mine_a, mine_b = wide_mine[real_at, :], wide_mine[imag_at, :]
    left = (jnp.concatenate([mine_a, mine_b], axis=0).astype(jnp.bfloat16),
            jnp.concatenate([mine_b, -mine_a], axis=0).astype(jnp.bfloat16))
    flat = csd_ref.reshape(rows * 2 * tiles, 128)
    for c in range(0, tiles, 2):
        right = jnp.concatenate([
            jnp.concatenate([wide[c, real_at, :], wide[c, imag_at, :]], axis=0),
            jnp.concatenate([wide[c + 1, real_at, :], wide[c + 1, imag_at, :]], axis=0),
        ], axis=1).astype(jnp.bfloat16)
        for p in range(2):
            value = lax.dot_general(left[p], right, over_rows, preferred_element_type=jnp.float32) * scale
            for u in range(2):
                flat[pl.ds(2 * (c + u) + p, rows, stride=2 * tiles), :] = value[:rows, u * 128 : (u + 1) * 128]

    ya, yb = applied[real_at, :], applied[imag_at, :]
    y_real = ya[:, :count] - yb[:, count:]
    y_imag = yb[:, :count] + ya[:, count:]
    y = jnp.concatenate([y_real, y_imag], axis=0)
    turned = jnp.concatenate([y_imag, -y_real], axis=0)
    for p, part in enumerate((y, turned)):
        held[...] = scale * lax.dot_general(
            part, y, over_rows, precision=lax.Precision.HIGHEST, preferred_element_type=jnp.float32)
        share = psd_ref.shape[1]
        psd_ref[p] = held[pl.ds(t * share, share), :]


def csd_aligned(scale, own, all_ref, loads_ref, csd_ref, psd_ref, wide, applied, held):
    csd_kernel(scale, own, all_ref, loads_ref, None, csd_ref, psd_ref, wide, None, applied, held)


def per_device(records, bins, loads):
    times = lax.axis_size("tm")
    t = lax.axis_index("tm")
    own, (_, count, rows) = bins.shape[0], loads.shape
    gathered, all_loads = gather_spectra(records, bins, loads)
    _, segs, _, cols = gathered.shape
    everything = gathered.reshape(-1, cols)
    aligned = rows == 128
    if rows % 128:
        whole = all_loads.transpose(1, 0, 2).reshape(2 * count, cols)
    else:
        whole = all_loads
    operands = [everything, whole]
    if not aligned:
        mine = lax.dynamic_slice_in_dim(everything, t * rows, rows, 1)
        operands.append(jnp.pad(mine, ((0, 0), (0, -rows % 128))))
    scale = float(1.0 / (segs * times * np.sum(window_of() ** 2)))
    tiles = cols // 128
    total, share = everything.shape[0], count // times
    full = lambda shape: pl.BlockSpec(shape, lambda b: (0, 0))
    csd, psd = pl.pallas_call(
        functools.partial(csd_aligned if aligned else csd_kernel, scale, own),
        grid=(own,),
        out_shape=(
            jax.ShapeDtypeStruct((rows, own, 2 * tiles, 128), jnp.float32),
            jax.ShapeDtypeStruct((2, own, share, count), jnp.float32),
        ),
        in_specs=[full(operand.shape) for operand in operands],
        out_specs=(
            pl.BlockSpec((rows, None, 2 * tiles, 128), lambda b: (0, b, 0, 0)),
            pl.BlockSpec((2, None, share, count), lambda b: (0, b, 0, 0)),
        ),
        scratch_shapes=[
            pltpu.VMEM((tiles, total, 128), jnp.float32),
            *([] if aligned else [pltpu.VMEM(operands[2].shape, jnp.float32)]),
            pltpu.VMEM((total, 2 * count), jnp.float32),
            pltpu.VMEM((count, count), jnp.float32),
        ],
        compiler_params=pltpu.CompilerParams(vmem_limit_bytes=56 * MIB),
        name="csd",
    )(*operands)
    csd = csd.reshape(rows, own, tiles, 2, 128).transpose(0, 1, 3, 2, 4).reshape(rows, own, 2, cols)
    return (csd, psd)


def solution(mesh):
    placed = (P("tm", "freq"), P("freq"), P(None, None, "tm"))
    return jax.shard_map(
        per_device,
        mesh=mesh,
        in_specs=placed,
        out_specs=(P("tm", "freq", None, None), P(None, "freq", "tm", None)),
        check_vma=False,
    )
```
